32 devices in a mesh: dp: 16 (over z, y, core), tensor: 2 (over x).
Axes of the slice: x: 2, y: 2, z: 4, core: 2. Of those that a mesh axis runs over, the one named last changes fastest.
Arguments:
- block_in: bfloat16 [16384, 1024], P(('dp', 'tensor')), may hold values from -6 to 6
- norm_gain: float32 [1024], replicated, may hold values from 0.25 to 1.75
- proj_gate: bfloat16 [1024, 2048], P('dp', 'tensor'), may hold values from -0.1875 to 0.1875
- proj_value: bfloat16 [1024, 2048], P('dp', 'tensor'), may hold values from -0.1875 to 0.1875
- proj_step: bfloat16 [1024, 32], P('dp', 'tensor'), may hold values from -0.1875 to 0.1875
- proj_bc: bfloat16 [1024, 256], P('dp'), may hold values from -0.1875 to 0.1875
- conv_value: float32 [5, 2048], P(None, 'tensor'), may hold values from -2 to 2
- conv_bc: float32 [5, 256], replicated, may hold values from -2 to 2
- head_params: float32 [3, 32], P(None, 'tensor'), may hold values from -6 to 2.5, as said below
- gate_gain: float32 [2048], P('tensor'), may hold values from 0.25 to 1.75
- proj_out: bfloat16 [2048, 1024], P('tensor', 'dp'), may hold values from -0.125 to 0.125
- grad_out: bfloat16 [16384, 1024], P(('dp', 'tensor')), may hold values from -6 to 6
Outputs:
- block_out: bfloat16 [16384, 1024], P(('dp', 'tensor'))
- grad_in: bfloat16 [16384, 1024], P(('dp', 'tensor'))
- grad_norm_gain: float32 [1024], replicated
- grad_proj_gate: float32 [1024, 2048], P('dp', 'tensor')
- grad_proj_value: float32 [1024, 2048], P('dp', 'tensor')
- grad_proj_step: float32 [1024, 32], P('dp', 'tensor')
- grad_proj_bc: float32 [1024, 256], P('dp')
- grad_conv_value: float32 [5, 2048], P(None, 'tensor')
- grad_conv_bc: float32 [5, 256], replicated
- grad_head_params: float32 [3, 32], P(None, 'tensor')
- grad_gate_gain: float32 [2048], P('tensor')
- grad_proj_out: float32 [2048, 1024], P('tensor', 'dp')
The draws below stay inside these ranges and needn't reach their ends.
Inputs may be any that keep to these rules, and one draw needn't show every extreme that they name: `head_params`: row 0 is added to the step before the softplus, row 1 is the logarithm of the decay rate, row 2 is the skip factor.
All inputs are finite; a program needn't handle non-finite values.
Results may differ from the reference program's by a relative error of at most 0.02.
Values may be sent and summed in bfloat16 or wider, within the bound.
A program may use at most 192 MiB of HBM per device.

```python
import jax
import jax.numpy as jnp
from jax import lax

D = 1024
HEADS = 32
STATE = 128
CONV = 4
SPAN = 256
SEQ_LEN = 1024
INNER = 2048
TOKENS = 16384


def draw_head_params(key, part):
    key = jax.random.fold_in(key, 7)
    subkeys = jax.random.split(key, 3)
    bias_row = jax.random.uniform(subkeys[0], (HEADS,), jnp.float32, -5.0, -1.0)
    rate_row = jax.random.uniform(subkeys[1], (HEADS,), jnp.float32, 0.0, 2.5)
    skip_row = jax.random.uniform(subkeys[2], (HEADS,), jnp.float32, 0.5, 1.5)
    return jnp.stack([bias_row, rate_row, skip_row])


def raised(array, key, source, target, shards_of, factor):
    def block_of(dim):
        return (jnp.arange(array.shape[dim]) // (array.shape[dim] // shards_of)).reshape((-1,) + (1,) * (array.ndim - 1 - dim))

    first = jax.random.permutation(key, shards_of)[block_of(target)]
    far = (block_of(target) + shards_of // 2) % shards_of
    return jnp.where((block_of(source) == first) | (block_of(source) == far), factor * array, array)


def level_of(key, dims, cuts, smallest, largest):
    def one(axis_at, blocks):
        heights = jax.random.uniform(jax.random.fold_in(jax.random.fold_in(key, 6), axis_at), (blocks,), jnp.float32, smallest / len(cuts), largest / len(cuts))
        return jnp.repeat(jnp.exp(heights), dims[axis_at] // blocks).reshape((-1,) + (1,) * (len(dims) - axis_at - 1))

    factor_of = one(*cuts[0])
    for cut in cuts[1:]:
        factor_of = factor_of * one(*cut)
    return factor_of


def normal_values(rng, shape, scale, reach, pieces=(), held_as=jnp.bfloat16):
    gain = level_of(rng, shape, pieces, -0.22, 0.18) if pieces else 1.0
    values = jax.random.normal(rng, shape, jnp.float32) * scale * gain
    return jnp.minimum(jnp.maximum(values, -reach), reach).astype(held_as)


def gaussian_with(stream_key, shape, scale, limit, cuts, heavy, kind=jnp.bfloat16):
    values = scale * jax.random.normal(stream_key, shape, jnp.float32)
    if cuts:
        values = values * level_of(stream_key, shape, cuts, -0.22, 0.18)
    return jnp.clip(raised(values, jax.random.fold_in(stream_key, 3), *heavy), -limit, limit).astype(kind)


def setup_inputs(seed: int = 0) -> dict:
    key_of = jax.random.split(jax.random.key(seed), 13)
    return {
        "block_in": gaussian_with(key_of[0], (TOKENS, D), 1.0, 6.0, ((0, 32),), (0, 1, 32, 2.75)),
        "norm_gain": jnp.clip(1.0 + 0.15 * jax.random.normal(key_of[1], (D,), jnp.float32), 0.25, 1.75),
        "proj_gate": normal_values(key_of[2], (D, INNER), D ** -0.5, 0.1875, ((0, 16), (1, 2))),
        "proj_value": normal_values(key_of[3], (D, INNER), D ** -0.5, 0.1875, ((0, 16), (1, 2))),
        "proj_step": normal_values(key_of[4], (D, HEADS), D ** -0.5, 0.1875, ((0, 16), (1, 2))),
        "proj_bc": normal_values(key_of[5], (D, 2 * STATE), D ** -0.5, 0.1875, ((0, 16),)),
        "conv_value": normal_values(key_of[6], (CONV + 1, INNER), 0.5, 2.0, ((1, 2),), jnp.float32),
        "conv_bc": normal_values(key_of[7], (CONV + 1, 2 * STATE), 0.5, 2.0, (), jnp.float32),
        "head_params": draw_head_params(jax.random.fold_in(key_of[12], 71), 0),
        "gate_gain": jnp.clip(1.0 + 0.15 * jax.random.normal(key_of[9], (INNER,), jnp.float32), 0.25, 1.75),
        "proj_out": normal_values(key_of[10], (INNER, D), INNER ** -0.5, 0.125, ((0, 2), (1, 16))),
        "grad_out": gaussian_with(key_of[11], (TOKENS, D), 1.0, 6.0, ((0, 32),), (0, 1, 32, 2.75)),
    }


EPS = 1e-05
HIGH = lax.Precision.HIGHEST

@jax.custom_vjp
def low(v):
    return lax.optimization_barrier(v.astype(jnp.bfloat16)).astype(jnp.float32)

@jax.custom_vjp
def low_back(v):
    return v

def low_keep(v):
    return (low(v), None)

def low_pass(kept, grad):
    return (grad,)

def back_keep(v):
    return (v, None)

def back_low(kept, grad):
    return (low(grad),)
low.defvjp(low_keep, low_pass)
low_back.defvjp(back_keep, back_low)

def matmul(left, right):
    return jnp.dot(left, right, precision=HIGH, preferred_element_type=jnp.float32)

def causal_conv(signal, kernel_rows):
    extent = kernel_rows.shape[0] - 1
    length = signal.shape[1]
    padded = jnp.pad(signal, ((0, 0), (extent - 1, 0), (0, 0)))
    summed = kernel_rows[extent] + padded[:, 0:length, :] * kernel_rows[0]
    for offset in range(1, extent):
        summed = summed + padded[:, offset:offset + length, :] * kernel_rows[offset]
    return jax.nn.silu(summed)

def convolve(value_raw, bc_raw, conv_value, conv_bc):
    return (causal_conv(value_raw, conv_value), causal_conv(bc_raw, conv_bc))

def mixer(value_conv, bc_conv, step_raw, head_params, gate_raw):
    seq_count, seq_length, chan_count = value_conv.shape
    head_count = step_raw.shape[2]
    head_size = chan_count // head_count
    state_count = bc_conv.shape[2] // 2
    block_count = seq_length // SPAN
    step_size = jax.nn.softplus(step_raw + head_params[0])
    decay_rate = -jnp.exp(head_params[1])
    values = value_conv.reshape(seq_count, block_count, SPAN, head_count, head_size)
    in_keys = bc_conv[..., :state_count].reshape(seq_count, block_count, SPAN, state_count)
    out_reads = bc_conv[..., state_count:].reshape(seq_count, block_count, SPAN, state_count)
    head_steps = jnp.transpose(step_size.reshape(seq_count, block_count, SPAN, head_count), (0, 1, 3, 2))
    log_decay = jnp.cumsum(head_steps * decay_rate[:, None], axis=3)
    causal = jnp.arange(SPAN)[:, None] >= jnp.arange(SPAN)[None, :]
    spread = log_decay[..., :, None] - log_decay[..., None, :]
    decay_mat = jnp.where(causal, jnp.exp(jnp.where(causal, spread, 0.0)), 0.0)
    intersection = jnp.einsum('skin,skjn->skij', out_reads, in_keys, precision=HIGH)
    mixing = intersection[:, :, None] * decay_mat * head_steps[..., None, :]
    inside = jnp.einsum('skhij,skjhp->skihp', mixing, values, precision=HIGH)
    tail_weight = jnp.exp(log_decay[..., -1:] - log_decay) * head_steps
    local_state = jnp.einsum('skhj,skjhp,skjn->skhpn', tail_weight, values, in_keys, precision=HIGH)
    block_fade = jnp.exp(log_decay[..., -1])

    def advance(carried, inputs):
        local_piece, factor = inputs
        return (carried * factor[..., None, None] + local_piece, carried)
    start_state = jnp.zeros((seq_count, head_count, head_size, state_count), local_state.dtype)
    unused, before = lax.scan(advance, start_state, (jnp.moveaxis(local_state, 1, 0), jnp.moveaxis(block_fade, 1, 0)))
    before = jnp.moveaxis(before, 0, 1)
    carried_in = jnp.einsum('skin,skhpn->skihp', out_reads, before, precision=HIGH)
    growth = jnp.transpose(jnp.exp(log_decay), (0, 1, 3, 2))[..., None]
    output = inside + carried_in * growth + head_params[2][:, None] * values
    return output.reshape(seq_count, seq_length, chan_count) * jax.nn.silu(gate_raw)

def forward(block_in, norm_gain, proj_gate, proj_value, proj_step, proj_bc, conv_value, conv_bc, head_params, gate_gain, proj_out):
    inverse = lax.rsqrt(lax.optimization_barrier(jnp.mean(block_in * block_in, axis=1, keepdims=True)) + EPS)
    normed = low(block_in * inverse * norm_gain)
    gate_raw = low_back(matmul(normed, proj_gate))
    value_raw = low_back(matmul(normed, proj_value))
    step_raw = low_back(matmul(normed, proj_step))
    bc_raw = low_back(matmul(normed, proj_bc))
    value_conv, bc_conv = convolve(value_raw[None], bc_raw[None], conv_value, conv_bc)
    gated = mixer(low(value_conv), low(bc_conv), step_raw[None], head_params, gate_raw[None])[0]
    scale = lax.rsqrt(lax.optimization_barrier(jnp.mean(gated * gated, axis=1, keepdims=True)) + EPS)
    lifted = low(gated * gate_gain)
    branch = low_back(matmul(lifted, proj_out))
    return block_in + scale * branch

def reference(block_in, norm_gain, proj_gate, proj_value, proj_step, proj_bc, conv_value, conv_bc, head_params, gate_gain, proj_out, grad_out):
    weights = (norm_gain, proj_gate.astype(jnp.float32), proj_value.astype(jnp.float32), proj_step.astype(jnp.float32), proj_bc.astype(jnp.float32), conv_value, conv_bc, head_params, gate_gain, proj_out.astype(jnp.float32))
    seq_total = TOKENS // SEQ_LEN
    inputs_seq = block_in.astype(jnp.float32).reshape(seq_total, SEQ_LEN, D)
    cot_seq = grad_out.astype(jnp.float32).reshape(seq_total, SEQ_LEN, D)

    def one_sequence(totals, seq_pair):
        seq_in, seq_cot = seq_pair
        result, pullback = jax.vjp(forward, seq_in, *weights)
        grads = pullback(seq_cot)
        return (tuple((summed + fresh for summed, fresh in zip(totals, grads[1:]))), (result, grads[0]))
    start_totals = tuple((jnp.zeros_like(member) for member in weights))
    totals, (outs_seq, grads_seq) = lax.scan(one_sequence, start_totals, (inputs_seq, cot_seq))
    grad_norm, grad_gate_w, grad_value_w, grad_step_w, grad_bc_w, grad_conv_v, grad_conv_b, grad_heads, grad_gain_g, grad_out_w = totals
    return (outs_seq.reshape(TOKENS, D).astype(jnp.bfloat16), grads_seq.reshape(TOKENS, D).astype(jnp.bfloat16), grad_norm, grad_gate_w, grad_value_w, grad_step_w, grad_bc_w, grad_conv_v, grad_conv_b, grad_heads, grad_gain_g, grad_out_w)
```

```python
import jax
import jax.numpy as jnp
from jax import lax
from jax.experimental import pallas as pl
from jax.experimental.pallas import tpu as pltpu
from jax.sharding import PartitionSpec as P

SPAN = 256
SEQ_LEN = 1024
INNER = 2048


EPS = 1e-05
STATE = 128
VMEM_BYTES = 56 * 1024 * 1024


def causal_conv(signal, kernel_rows):
    extent = kernel_rows.shape[0] - 1
    length = signal.shape[1]
    padded = jnp.pad(signal, ((0, 0), (extent - 1, 0), (0, 0)))
    summed = kernel_rows[extent] + padded[:, 0:length, :] * kernel_rows[0]
    for offset in range(1, extent):
        summed = summed + padded[:, offset : offset + length, :] * kernel_rows[offset]
    return jax.nn.silu(summed)


def convolve(value_raw, bc_raw, conv_value, conv_bc):
    return (causal_conv(value_raw, conv_value), causal_conv(bc_raw, conv_bc))


def spread_matrix(head_count, chan_count):
    size = chan_count // head_count
    rows = lax.broadcasted_iota(jnp.int32, (head_count, chan_count), 0)
    cols = lax.broadcasted_iota(jnp.int32, (head_count, chan_count), 1)
    first = rows * size
    return jnp.where((cols >= first) & (cols < first + size), 1.0, 0.0)


def dot(left, right, dims, precision=None):
    return lax.dot_general(
        left, right, (dims, ((), ())), precision=precision, preferred_element_type=jnp.float32
    )


MM = ((1,), (0,))
TM = ((0,), (0,))
MT = ((1,), (1,))
FULL = lax.Precision.HIGHEST


def widen(table, spread):
    high = table.astype(jnp.bfloat16)
    low = (table - high.astype(jnp.float32)).astype(jnp.bfloat16)
    return dot(high, spread, MM) + dot(low, spread, MM)


def causal_mask():
    rows = lax.broadcasted_iota(jnp.int32, (SPAN, SPAN), 0)
    cols = lax.broadcasted_iota(jnp.int32, (SPAN, SPAN), 1)
    return rows >= cols


def scan_forward_kernel(v_ref, b_ref, c_ref, lc_ref, lr_ref, dt_ref, skip_ref, y_ref, s_ref, state):
    head_count, chan_count = lc_ref.shape[1], v_ref.shape[1]
    size = chan_count // head_count
    group = max(1, 128 // size)

    @pl.when(pl.program_id(1) == 0)
    def _():
        state[...] = jnp.zeros_like(state)

    spread_full = spread_matrix(head_count, chan_count)
    spread = spread_full.astype(jnp.bfloat16)
    values = v_ref[...].astype(jnp.float32)
    b, c, lc = b_ref[...], c_ref[...], lc_ref[...]
    start = state[...]
    s_ref[0] = start
    last = lc[SPAN - 1 : SPAN, :]
    stepped = (widen(dt_ref[...], spread) * values).astype(jnp.bfloat16)
    grow = dot(jnp.exp(lc).astype(jnp.bfloat16), spread, MM)
    base = dot(c, start.astype(jnp.bfloat16), MM) * grow + skip_ref[...] * values
    inter = jnp.where(causal_mask(), dot(c, b, MT), 0.0)
    for lead in range(0, head_count, group):
        parts = []
        for h in range(lead, lead + group):
            decay = jnp.exp(jnp.minimum(lc[:, h : h + 1] - lr_ref[h : h + 1, :], 0.0))
            parts.append(
                dot((inter * decay).astype(jnp.bfloat16), stepped[:, h * size : (h + 1) * size], MM)
            )
        lanes = slice(lead * size, (lead + group) * size)
        y_ref[:, lanes] = base[:, lanes] + jnp.concatenate(parts, axis=1)
    tail = dot(jnp.exp(last - lc).astype(jnp.bfloat16), spread, MM)
    weighted = (tail * stepped.astype(jnp.float32)).astype(jnp.bfloat16)
    fade = dot(jnp.exp(last), spread_full, MM, FULL)
    state[...] = start * fade + dot(b, weighted, TM)


def scan_backward_kernel(
    v_ref, b_ref, c_ref, lc_ref, lr_ref, dt_ref, skip_ref, gy_ref, y_ref, s_ref,
    gv_ref, gb_ref, gc_ref, direct_ref, decay_ref, skipped_ref, adjoint,
):
    head_count, chan_count = lc_ref.shape[1], v_ref.shape[1]
    size = chan_count // head_count
    group = max(1, 128 // size)

    @pl.when(pl.program_id(1) == 0)
    def _():
        adjoint[...] = jnp.zeros_like(adjoint)

    spread_full = spread_matrix(head_count, chan_count)
    spread = spread_full.astype(jnp.bfloat16)
    values = v_ref[...].astype(jnp.float32)
    b, c, lc, gy = b_ref[...], c_ref[...], lc_ref[...], gy_ref[...]
    gy_wide = gy.astype(jnp.float32)
    skip = skip_ref[...]
    start = s_ref[0]
    later = adjoint[...]
    later_low = later.astype(jnp.bfloat16)
    last = lc[SPAN - 1 : SPAN, :]
    steps = widen(dt_ref[...], spread)
    stepped = (steps * values).astype(jnp.bfloat16)
    stepped_wide = stepped.astype(jnp.float32)
    grow = dot(jnp.exp(lc).astype(jnp.bfloat16), spread, MM)
    tail = dot(jnp.exp(last - lc).astype(jnp.bfloat16), spread, MM)
    fade = dot(jnp.exp(last), spread_full, MM, FULL)
    grown = (gy_wide * grow).astype(jnp.bfloat16)
    weighted = (tail * stepped_wide).astype(jnp.bfloat16)
    from_later = dot(b, later_low, MM) * tail
    mask = causal_mask()
    inter = jnp.where(mask, dot(c, b, MT), 0.0)
    mixed = jnp.zeros((SPAN, SPAN), jnp.float32)
    pieces = []
    for lead in range(0, head_count, group):
        for h in range(lead, lead + group):
            lanes = slice(h * size, (h + 1) * size)
            decay = jnp.exp(jnp.minimum(lc[:, h : h + 1] - lr_ref[h : h + 1, :], 0.0))
            pieces.append(dot((inter * decay).astype(jnp.bfloat16), gy[:, lanes], TM))
            mixed = mixed + dot(gy[:, lanes], stepped[:, lanes], MT) * decay
    grad_stepped = from_later + jnp.concatenate(pieces, axis=1)
    gv_ref[...] = steps * grad_stepped + skip * gy_wide
    mixed_low = jnp.where(mask, mixed, 0.0).astype(jnp.bfloat16)
    gc_ref[...] = dot(mixed_low, b, MM) + dot(grown, start.astype(jnp.bfloat16), MT)
    gb_ref[...] = dot(mixed_low, c, TM) + dot(weighted, later_low, MT)
    direct_ref[...] = dot(values * grad_stepped, spread_full, MT, FULL)
    skipped_ref[...] = dot(values * gy_wide, spread_full, MT, FULL)
    ends = jnp.sum(later * start, axis=0, keepdims=True) * fade + jnp.sum(
        stepped_wide * from_later, axis=0, keepdims=True
    )
    balance = gy_wide * (y_ref[...] - skip * values) - stepped_wide * grad_stepped
    rows = lax.broadcasted_iota(jnp.int32, balance.shape, 0)
    balance = balance + jnp.where(rows == SPAN - 1, ends, 0.0)
    onward = jnp.where(mask, 1.0, 0.0)
    decay_ref[...] = dot(onward, dot(balance, spread_full, MT, FULL), TM, FULL)
    adjoint[...] = later * fade + dot(c, grown, TM)


def scan_specs(seq_count, block_count, head_count, chan_count, backward):
    def at(s, k):
        return s * block_count + (block_count - 1 - k if backward else k)

    def tall(width):
        return pl.BlockSpec((SPAN, width), lambda s, k: (at(s, k), 0))

    inputs = [
        tall(chan_count),
        pl.BlockSpec((SPAN, STATE), lambda s, k: (at(s, k), 0)),
        pl.BlockSpec((SPAN, STATE), lambda s, k: (at(s, k), 1)),
        tall(head_count),
        pl.BlockSpec((head_count, SPAN), lambda s, k: (0, at(s, k))),
        tall(head_count),
        pl.BlockSpec((1, chan_count), lambda s, k: (0, 0)),
    ]
    states = pl.BlockSpec((1, STATE, chan_count), lambda s, k: (at(s, k), 0, 0))
    return inputs, tall, states


def scan_forward(values, bc, lc, lr, dt, skip):
    rows, chan_count = values.shape
    head_count = dt.shape[1]
    seq_count, block_count = rows // SEQ_LEN, SEQ_LEN // SPAN
    inputs, tall, states = scan_specs(seq_count, block_count, head_count, chan_count, False)
    return pl.pallas_call(
        scan_forward_kernel,
        grid=(seq_count, block_count),
        in_specs=inputs,
        out_specs=[tall(chan_count), states],
        out_shape=[
            jax.ShapeDtypeStruct((rows, chan_count), jnp.float32),
            jax.ShapeDtypeStruct((rows // SPAN, STATE, chan_count), jnp.float32),
        ],
        scratch_shapes=[pltpu.VMEM((STATE, chan_count), jnp.float32)],
        compiler_params=pltpu.CompilerParams(vmem_limit_bytes=VMEM_BYTES),
        cost_estimate=pl.CostEstimate(
            flops=12 * rows * SPAN * chan_count,
            bytes_accessed=14 * rows * chan_count,
            transcendentals=rows * SPAN * head_count,
        ),
        name="scan_forward",
    )(values, bc, bc, lc, lr, dt, skip)


def scan_backward(values, bc, lc, lr, dt, skip, grad_y, y, states_in):
    rows, chan_count = values.shape
    head_count = dt.shape[1]
    seq_count, block_count = rows // SEQ_LEN, SEQ_LEN // SPAN
    inputs, tall, states = scan_specs(seq_count, block_count, head_count, chan_count, True)
    heads = jax.ShapeDtypeStruct((rows, head_count), jnp.float32)
    return pl.pallas_call(
        scan_backward_kernel,
        grid=(seq_count, block_count),
        in_specs=inputs + [tall(chan_count), tall(chan_count), states],
        out_specs=[tall(chan_count), tall(STATE), tall(STATE)] + [tall(head_count)] * 3,
        out_shape=[
            jax.ShapeDtypeStruct((rows, chan_count), jnp.float32),
            jax.ShapeDtypeStruct((rows, STATE), jnp.float32),
            jax.ShapeDtypeStruct((rows, STATE), jnp.float32),
            heads,
            heads,
            heads,
        ],
        scratch_shapes=[pltpu.VMEM((STATE, chan_count), jnp.float32)],
        compiler_params=pltpu.CompilerParams(vmem_limit_bytes=VMEM_BYTES),
        cost_estimate=pl.CostEstimate(
            flops=36 * rows * SPAN * chan_count,
            bytes_accessed=20 * rows * chan_count,
            transcendentals=rows * SPAN * head_count,
        ),
        name="scan_backward",
    )(values, bc, bc, lc, lr, dt, skip, grad_y, y, states_in)


def swap_with(array, axis, bit):
    count = lax.axis_size(axis)
    return lax.ppermute(array, axis, [(i, i ^ bit) for i in range(count)])


def scatter_rows(array, axis):
    count = lax.axis_size(axis)
    here = lax.axis_index(axis)
    width = array.shape[1]
    held = array.astype(jnp.bfloat16).reshape(count, array.shape[0] // count, width)
    bit = 1
    while bit < count:
        pairs = held.reshape(held.shape[0] // 2, 2, *held.shape[1:])
        mine = (here // bit) % 2
        away = lax.dynamic_index_in_dim(pairs, 1 - mine, 1, keepdims=False)
        kept = lax.dynamic_index_in_dim(pairs, mine, 1, keepdims=False)
        summed = kept.astype(jnp.float32) + swap_with(away, axis, bit).astype(jnp.float32)
        bit *= 2
        held = summed.astype(jnp.bfloat16) if bit < count else summed
    return held[0].astype(jnp.float32)


def gather_rows(array, axis):
    count = lax.axis_size(axis)
    here = lax.axis_index(axis)
    rows, width = array.shape
    held = array[None]
    bit = count // 2
    while bit:
        other = swap_with(held, axis, bit)
        first = (here // bit) % 2 == 0
        held = jnp.stack([jnp.where(first, held, other), jnp.where(first, other, held)], axis=1)
        held = held.reshape(-1, rows, width)
        bit //= 2
    return held.reshape(count * rows, width)


def sum_all(array, axis):
    bit = 1
    while bit < lax.axis_size(axis):
        array = array + swap_with(array, axis, bit)
        bit *= 2
    return array


def rounded(matrix):
    return lax.optimization_barrier(matrix.astype(jnp.bfloat16)).astype(jnp.float32)


def lead_contract(left, right):
    return lax.dot_general(
        left, right, (((0,), (0,)), ((), ())), preferred_element_type=jnp.float32
    )


def tail_contract(left, right):
    return lax.dot_general(
        left, right, (((1,), (1,)), ((), ())), preferred_element_type=jnp.float32
    )


def shards(
    block_in,
    norm_gain,
    proj_gate,
    proj_value,
    proj_step,
    proj_bc,
    conv_value,
    conv_bc,
    head_params,
    gate_gain,
    proj_out,
    grad_out,
):
    tensor_count = lax.axis_size("tensor")
    own_rows = block_in.shape[0]
    all_rows = own_rows * tensor_count
    seq_count = all_rows // SEQ_LEN
    first_row = lax.axis_index("tensor") * own_rows
    model_width = block_in.shape[1]
    block_wide = block_in.astype(jnp.float32)
    inverse = lax.rsqrt(jnp.mean(block_wide * block_wide, axis=1, keepdims=True) + EPS)
    normed = (block_wide * inverse * norm_gain).astype(jnp.bfloat16)
    step_count, bc_count = proj_step.shape[1], proj_bc.shape[1]
    narrow = jnp.concatenate(
        [proj_bc, jnp.pad(proj_step, ((0, 0), (0, -step_count % 128)))], axis=1
    )
    full_narrow = gather_rows(narrow, "dp")
    gathered = gather_rows(normed, "tensor")
    full_value = gather_rows(proj_value, "dp")
    full_gate = gather_rows(proj_gate, "dp")
    full_out_t = gather_rows(proj_out.T, "dp")
    full_bc = full_narrow[:, :bc_count]
    full_step = full_narrow[:, bc_count : bc_count + step_count]
    narrow_raw = jnp.dot(gathered, full_narrow, preferred_element_type=jnp.float32)
    bc_raw = narrow_raw[:, :bc_count]
    step_raw = narrow_raw[:, bc_count : bc_count + step_count]
    value_raw = jnp.dot(gathered, full_value, preferred_element_type=jnp.float32)
    gate_raw = jnp.dot(gathered, full_gate, preferred_element_type=jnp.float32)

    def by_sequence(matrix):
        return matrix.reshape(seq_count, SEQ_LEN, matrix.shape[1])

    conv_pair, conv_back = jax.vjp(
        convolve, by_sequence(value_raw), by_sequence(bc_raw), conv_value, conv_bc
    )
    value_conv = conv_pair[0].reshape(all_rows, -1).astype(jnp.bfloat16)
    bc_conv = conv_pair[1].reshape(all_rows, -1).astype(jnp.bfloat16)
    head_size = value_conv.shape[1] // step_count
    step_in = step_raw + head_params[0]
    steps = jax.nn.softplus(step_in)
    rate = -jnp.exp(head_params[1])
    logs = jnp.cumsum((steps * rate).reshape(-1, SPAN, step_count), axis=1)
    logs = logs.reshape(all_rows, step_count)
    scan_inputs = (
        value_conv,
        bc_conv,
        logs,
        logs.T,
        steps,
        jnp.repeat(head_params[2], head_size)[None],
    )
    y, states = scan_forward(*scan_inputs)
    sigma = jax.nn.sigmoid(gate_raw)
    opened = gate_raw * sigma
    gated = y * opened
    squares = jnp.sum(gated * gated, axis=1)
    lifted = (gated * gate_gain).astype(jnp.bfloat16)
    total_squares = lax.psum(squares, "tensor")
    scale_all = lax.rsqrt(total_squares / INNER + EPS)
    branch = scatter_rows(tail_contract(lifted, full_out_t), "tensor")
    scale = lax.dynamic_slice_in_dim(scale_all, first_row, own_rows, 0)
    block_out = (block_wide + scale[:, None] * branch).astype(jnp.bfloat16)
    cotangent = grad_out.astype(jnp.float32)
    slope_own = -0.5 * scale * scale * scale * jnp.sum(cotangent * branch, axis=1)
    sent = (scale[:, None] * cotangent).astype(jnp.bfloat16)
    branch_grad, slope = (
        gather_rows(sent, "tensor"),
        lax.all_gather(slope_own.astype(jnp.bfloat16), "tensor", axis=0, tiled=True).astype(
            slope_own.dtype
        ),
    )
    grad_out_w = scatter_rows(lead_contract(branch_grad, lifted), "dp").T
    grad_lifted = jnp.dot(branch_grad, full_out_t, preferred_element_type=jnp.float32)
    grad_gate_gain = jnp.sum(grad_lifted * gated, axis=0)
    grad_gated = grad_lifted * gate_gain + 2.0 / INNER * slope[:, None] * gated
    grad_y = (grad_gated * opened).astype(jnp.bfloat16)
    gate_low = (grad_gated * y * sigma * (1.0 + gate_raw * (1.0 - sigma))).astype(jnp.bfloat16)
    grad_gate_w = scatter_rows(lead_contract(gathered, gate_low), "dp")
    grad_vconv, grad_b, grad_c, direct, decayed, skipped = scan_backward(
        *scan_inputs, grad_y, y, states
    )
    grad_bcconv = jnp.concatenate([grad_b, grad_c], axis=1)
    bit = 1
    while bit < tensor_count:
        low = lax.optimization_barrier(grad_bcconv.astype(jnp.bfloat16))
        grad_bcconv = low.astype(jnp.float32) + swap_with(low, "tensor", bit).astype(jnp.float32)
        bit *= 2
    grad_step = (direct + rate * decayed) * jax.nn.sigmoid(step_in)
    grad_heads = jnp.stack(
        [
            jnp.sum(grad_step, axis=0),
            jnp.sum(steps * decayed, axis=0) * rate,
            jnp.sum(skipped, axis=0),
        ]
    )
    grad_value_raw, grad_bc_raw, grad_conv_value, grad_conv_bc = conv_back(
        (by_sequence(grad_vconv), by_sequence(grad_bcconv))
    )

    def flat_low(array):
        return array.reshape(all_rows, array.shape[2]).astype(jnp.bfloat16)

    value_low = flat_low(grad_value_raw)
    step_low = grad_step.astype(jnp.bfloat16)
    bc_low = flat_low(grad_bc_raw)
    grad_value_w = scatter_rows(lead_contract(gathered, value_low), "dp")
    narrow_low = jnp.concatenate(
        [bc_low, jnp.pad(step_low, ((0, 0), (0, -step_count % 128)))], axis=1
    )
    grad_narrow_w = scatter_rows(lead_contract(gathered, narrow_low), "dp")
    grad_bc_w = grad_narrow_w[:, :bc_count]
    grad_step_w = grad_narrow_w[:, bc_count : bc_count + step_count]
    summed = tail_contract(gate_low, full_gate)
    summed = summed + tail_contract(value_low, full_value)
    grad_normed = scatter_rows(summed + tail_contract(step_low, full_step), "tensor")
    grad_normed = grad_normed + tail_contract(
        lax.dynamic_slice_in_dim(bc_low, first_row, own_rows, 0), full_bc
    )
    weighted = grad_normed * norm_gain
    own_gain = jnp.sum(grad_normed * block_wide * inverse, axis=0)
    inverse_cubed = inverse * inverse * inverse
    grad_in = (
        cotangent
        + inverse * weighted
        - block_wide
        * inverse_cubed
        * jnp.sum(weighted * block_wide, axis=1, keepdims=True)
        / model_width
    )
    small = (
        grad_conv_value.reshape(-1),
        grad_gate_gain,
        grad_conv_bc.reshape(-1),
        sum_all(own_gain, "tensor"),
        grad_heads.reshape(-1),
    )
    total = sum(part.shape[0] for part in small)
    packed = jnp.pad(jnp.concatenate(small), (0, -total % 1024)).reshape(-1, 128)
    packed = sum_all(packed, "dp").reshape(-1)
    edges = [0]
    for part in small:
        edges.append(edges[-1] + part.shape[0])
    flat = [packed[edges[i] : edges[i + 1]] for i in range(len(small))]
    conv_value_sum = flat[0].reshape(grad_conv_value.shape)
    gate_gain_sum = flat[1]
    conv_bc_sum = flat[2].reshape(grad_conv_bc.shape)
    grad_norm_gain = flat[3]
    heads_sum = flat[4].reshape(grad_heads.shape)
    return (
        block_out,
        grad_in.astype(jnp.bfloat16),
        grad_norm_gain,
        grad_gate_w,
        grad_value_w,
        grad_step_w,
        grad_bc_w,
        conv_value_sum,
        conv_bc_sum,
        heads_sum,
        gate_gain_sum,
        grad_out_w,
    )


def solution(mesh):
    return jax.shard_map(
        shards,
        mesh=mesh,
        in_specs=(
            P(("dp", "tensor"), None),
            P(),
            P("dp", "tensor"),
            P("dp", "tensor"),
            P("dp", "tensor"),
            P("dp", None),
            P(None, "tensor"),
            P(),
            P(None, "tensor"),
            P("tensor"),
            P("tensor", "dp"),
            P(("dp", "tensor"), None),
        ),
        out_specs=(
            P(("dp", "tensor"), None),
            P(("dp", "tensor"), None),
            P(),
            P("dp", "tensor"),
            P("dp", "tensor"),
            P("dp", "tensor"),
            P("dp", None),
            P(None, "tensor"),
            P(),
            P(None, "tensor"),
            P("tensor"),
            P("tensor", "dp"),
        ),
        check_vma=False,
    )
```
